128 devices in a mesh: wide: 16 (over x_hi, z, core), narrow: 8 (over x_lo, y).
Axes of the slice: x: 4 (x_hi: 2, x_lo: 2; x = x_hi * 2 + x_lo), y: 4, z: 4, core: 2. Of those that a mesh axis runs over, the one named last changes fastest.
Arguments:
- pair_elements: bfloat16 [2048, 16000], P(('wide', 'narrow')), may hold values from -2.5 to 2.5
- valence_index: int32 [2048], replicated, may hold values from 0 to 2399
- conduction_index: int32 [2048], replicated, may hold values from 0 to 9599
- val_energy: float32 [2400], replicated, may hold values from -12 to -0.5
- cond_energy: float32 [9600], replicated, may hold values from 0.5 to 20
- omegas: float32 [2], replicated, may hold values from 0.2 to 10
Outputs:
- response: float32 [2, 16000, 16000], P(None, 'wide', 'narrow')
The draws below stay inside these ranges and needn't reach their ends.
All inputs are finite; a program needn't handle non-finite values.
Results may differ from the reference program's by a relative error of at most 0.0028.
Values may be sent and summed in bfloat16 or wider, within the bound.
No kernel may reach another device: no remote copies, remote signals or barrier semaphores. Data moves between devices by JAX's collectives and lax.ppermute only.
A program may use at most 128 MiB of HBM per device.

```python
import math
import jax
import jax.numpy as jnp

NG = 16000
NV = 2400
NC = 9600
NF = 2
PAIRS = 2048


def touch_ends(drawn, own_key, least, high):
    spot = [jax.random.randint(jax.random.fold_in(own_key, axis), (), 0, length) for axis, length in enumerate(drawn.shape)]
    widest = drawn.shape.index(max(drawn.shape))
    beside = spot[:widest] + [(spot[widest] + 1) % drawn.shape[widest]] + spot[widest + 1:]
    return drawn.at[tuple(spot)].set(least).at[tuple(beside)].set(high)


def level_of(stream_key, dims, cuts, low, top_value):
    level, own = 1.0, jax.random.fold_in(stream_key, 6)
    for dim, blocks in cuts:
        heights = jnp.exp(jax.random.uniform(jax.random.fold_in(own, dim), (blocks,), jnp.float32, low / len(cuts), top_value / len(cuts)))
        level = level * jnp.repeat(heights, dims[dim] // blocks).reshape([-1 if axis == dim else 1 for axis in range(len(dims))])
    return level


def noise(rng, dims, spread, most, cuts=(), kind=jnp.bfloat16):
    level = level_of(rng, dims, cuts, -0.22, 0.18) if cuts else 1.0
    result = jax.random.normal(rng, dims, jnp.float32) * spread * level
    return jnp.minimum(jnp.maximum(result, -most), most).astype(kind)


def setup_inputs(seed: int = 0) -> dict:
    keys = jax.random.split(jax.random.key(seed), 7)
    pair_elements = noise(keys[0], (PAIRS, NG), 0.4, 2.5, ((0, 128),))
    valence_index = touch_ends(jax.random.randint(keys[1], (PAIRS,), 0, NV), jax.random.fold_in(keys[1], 1), 0, NV - 1).astype(jnp.int32)
    conduction_index = touch_ends(jax.random.randint(keys[2], (PAIRS,), 0, NC), jax.random.fold_in(keys[2], 1), 0, NC - 1).astype(jnp.int32)
    val_energy = jnp.clip(jax.random.uniform(keys[3], (NV,), jnp.float32, -12.0, -0.5), -12.0, -0.5)
    cond_energy = jnp.clip(jax.random.uniform(keys[4], (NC,), jnp.float32, 0.5, 20.0), 0.5, 20.0)
    omegas = jnp.clip(jnp.exp(jax.random.uniform(keys[5], (NF,), jnp.float32, math.log(0.2), math.log(10.0))), 0.2, 10.0)
    return {"pair_elements": pair_elements, "valence_index": valence_index, "conduction_index": conduction_index, "val_energy": val_energy, "cond_energy": cond_energy, "omegas": omegas}


def reference(pair_elements, valence_index, conduction_index, val_energy, cond_energy, omegas):
    energy_gap = jnp.take(cond_energy, conduction_index) - jnp.take(val_energy, valence_index)
    gap_row = energy_gap[None, :]
    weight = -4.0 * gap_row / (gap_row * gap_row + omegas[:, None] * omegas[:, None])
    scaled = (weight[:, :, None] * pair_elements[None, :, :]).astype(jnp.bfloat16)
    return jnp.einsum("fpg,ph->fgh", scaled.astype(jnp.float32), pair_elements.astype(jnp.float32))
```

```python
import functools
import jax
import jax.numpy as jnp
from jax import lax
from jax.experimental import pallas as pl
from jax.experimental.pallas import tpu as pltpu
from jax.sharding import Mesh, PartitionSpec as P

ROWS = 1000
COLUMNS = 2000
WIDE, NARROW, OWN = 16, 8, 16
PAIRS = WIDE * NARROW * OWN
KEEP = NARROW * OWN
CHUNK = WIDE * OWN
TILE = 512
PADDED = -(-COLUMNS // TILE) * TILE


def spread(table):
    rows = -(-table.shape[0] // 1024) * 8
    return jnp.pad(table, (0, rows * 128 - table.shape[0])).reshape(rows, 128)


def weights_kernel(valence_ref, conduction_ref, val_ref, cond_ref, omegas_ref, out_ref):
    def lookup(index, table):
        high, low = index // 128, index % 128
        block = lax.broadcasted_iota(jnp.int32, (table.shape[0], PAIRS), 0)
        picked = lax.dot_general(
            table,
            (block == high).astype(jnp.float32),
            (((0,), (0,)), ((), ())),
            precision=lax.Precision.HIGHEST,
            preferred_element_type=jnp.float32,
        )
        lane = lax.broadcasted_iota(jnp.int32, (128, PAIRS), 0)
        return jnp.sum(jnp.where(lane == low, picked, 0.0), axis=0, keepdims=True)

    gap = lookup(conduction_ref[...], cond_ref[...]) - lookup(valence_ref[...], val_ref[...])
    for f in range(2):
        omega = omegas_ref[f]
        out_ref[f : f + 1, :] = -4.0 * gap / (gap * gap + omega * omega)


def pair_weights(valence_index, conduction_index, val_energy, cond_energy, omegas):
    def order(index):
        return index.reshape(WIDE, NARROW, OWN).transpose(1, 0, 2).reshape(1, PAIRS)

    vmem = pl.BlockSpec(memory_space=pltpu.VMEM)
    return pl.pallas_call(
        weights_kernel,
        out_shape=jax.ShapeDtypeStruct((2, PAIRS), jnp.float32),
        in_specs=[vmem] * 4 + [pl.BlockSpec(memory_space=pltpu.SMEM)],
        out_specs=vmem,
        compiler_params=pltpu.CompilerParams(vmem_limit_bytes=24 << 20),
        name="weights",
    )(order(valence_index), order(conduction_index), spread(val_energy), spread(cond_energy), omegas)


def product_kernel(place_ref, weight_ref, rows_ref, *refs):
    blocks = refs[:WIDE]
    out_ref, rows, scaled, columns, rows_sem, block_sem = refs[WIDE:]
    j = pl.program_id(0)

    def row_copy(n):
        return pltpu.make_async_copy(rows_ref.at[n], rows.at[n], rows_sem.at[n])

    def block_copy(k):
        return pltpu.make_async_copy(blocks[k], columns.at[:, place_ref[k]], block_sem.at[k])

    @pl.when(j == 0)
    def _():
        for n in range(NARROW):
            row_copy(n).start()
        for k in range(WIDE):
            block_copy(k).start()
        for n in range(NARROW):
            row_copy(n).wait()
            part = rows[n].astype(jnp.float32)
            for f in range(2):
                lanes = slice(n * CHUNK, (n + 1) * CHUNK)
                scaled[f, :, lanes] = (part * weight_ref[f : f + 1, lanes]).astype(jnp.bfloat16)
        for k in range(WIDE):
            block_copy(k).wait()

    start = pl.multiple_of(j * TILE, TILE)
    right = columns[:, :, :, pl.ds(start, TILE)].reshape(PAIRS, TILE)
    for f in range(2):
        out_ref[f] = jnp.dot(scaled[f], right, preferred_element_type=jnp.float32)


def product(place, weight, rows, blocks):
    any_space = pl.BlockSpec(memory_space=pl.ANY)
    blocks = [b.reshape(NARROW, OWN, PADDED) for b in blocks]
    return pl.pallas_call(
        product_kernel,
        grid=(PADDED // TILE,),
        out_shape=jax.ShapeDtypeStruct((2, ROWS, COLUMNS), jnp.float32),
        in_specs=[pl.BlockSpec(memory_space=pltpu.SMEM), pl.BlockSpec(memory_space=pltpu.VMEM)]
        + [any_space] * (1 + WIDE),
        out_specs=pl.BlockSpec((2, ROWS, TILE), lambda j: (0, 0, j)),
        scratch_shapes=[
            pltpu.VMEM((NARROW, ROWS, CHUNK), jnp.bfloat16),
            pltpu.VMEM((2, ROWS, PAIRS), jnp.bfloat16),
            pltpu.VMEM((NARROW, WIDE, OWN, PADDED), jnp.bfloat16),
            pltpu.SemaphoreType.DMA((NARROW,)),
            pltpu.SemaphoreType.DMA((WIDE,)),
        ],
        compiler_params=pltpu.CompilerParams(vmem_limit_bytes=52 << 20),
        cost_estimate=pl.CostEstimate(
            flops=4 * ROWS * COLUMNS * PAIRS, bytes_accessed=28 << 20, transcendentals=0
        ),
        name="product",
    )(place, weight, rows, *blocks)


def step(value, axis, size, by):
    return lax.ppermute(value, axis, [(i, (i + by) % size) for i in range(size)])


def gather_columns(own):
    xh, z, c = lax.axis_index("xh"), lax.axis_index("z"), lax.axis_index("c")
    other = step(own, "xh", 2, 1)
    near = [own, other]
    up = [step(v, "z", 4, 1) for v in near]
    down = [step(v, "z", 4, -1) for v in near]
    far = [step(up[0], "z", 4, 1), step(down[1], "z", 4, -1)]
    mine = near + up + down + far
    theirs = [step(v, "c", 2, 1) for v in mine]
    places = []
    for core in (c, 1 - c):
        for k, shift in enumerate((0, 0, 3, 3, 1, 1, 2, 2)):
            places.append(((xh + k) % 2 * 4 + (z + shift) % 4) * 2 + core)
    return mine + theirs, jnp.stack(places).astype(jnp.int32)


def body(pair_elements, valence_index, conduction_index, val_energy, cond_energy, omegas):
    weight = pair_weights(valence_index, conduction_index, val_energy, cond_energy, omegas)
    row_part = lax.all_to_all(pair_elements, ("xh", "z", "c"), split_axis=1, concat_axis=0, tiled=True)
    rows = lax.all_gather(row_part.T, ("xl", "y"))
    slices = jnp.pad(pair_elements.reshape(OWN, NARROW, COLUMNS), ((0, 0), (0, 0), (0, PADDED - COLUMNS)))
    column_part = lax.all_to_all(slices.transpose(1, 0, 2), ("xl", "y"), split_axis=0, concat_axis=0, tiled=True)
    blocks, place = gather_columns(column_part)
    return product(place, weight, rows, blocks)


def solution(mesh):
    fine = Mesh(mesh.devices.reshape(2, 4, 2, 2, 4), ("xh", "z", "c", "xl", "y"))
    wide, narrow = ("xh", "z", "c"), ("xl", "y")
    return jax.shard_map(
        body,
        mesh=fine,
        in_specs=(P(wide + narrow, None), P(), P(), P(), P(), P()),
        out_specs=P(None, wide, narrow),
        check_vma=False,
    )
```

```python
import jax
import jax.numpy as jnp
from jax import lax
from jax.experimental import pallas as pl
from jax.experimental.pallas import tpu as pltpu
from jax.sharding import Mesh, PartitionSpec as P

ALL = ("xh", "z", "c", "xl", "y")
SIZES = (2, 4, 2, 2, 4)
ROWS = 1000
COLUMNS = 2000
GROUP = 8
OWN = 16
PAIRS = GROUP * GROUP * 2 * OWN
BLOCK = GROUP * 2 * OWN
PADDED = 2048
PANEL = 256
PANELS = PADDED // PANEL
HALF = 1024


def device(xh, z, c, xl, y):
    return (((xh % 2 * 4 + z % 4) * 2 + c) * 2 + xl % 2) * 4 + y % 4


def every():
    return [(xh, z, c, xl, y) for xh in range(2) for z in range(4) for c in range(2) for xl in range(2) for y in range(4)]


def move(value, to):
    return lax.ppermute(value, ALL, [(device(*d), device(*to(*d))) for d in every()])


def swap_cores(value):
    return move(value, lambda xh, z, c, xl, y: (xh, z, 1 - c, xl, y))


def swap_x(value):
    return move(value, lambda xh, z, c, xl, y: (xh, z, c, xl + 1, y) if c == 0 else (xh + 1, z, c, xl, y))


def ring(value, by):
    return move(value, lambda xh, z, c, xl, y: (xh, z, c, xl, y + by) if c == 0 else (xh, z + by, c, xl, y))


def spread(table):
    rows = -(-table.shape[0] // 1024) * 8
    return jnp.pad(table, (0, rows * 128 - table.shape[0])).reshape(rows, 128)


def weights_kernel(valence_ref, conduction_ref, val_ref, cond_ref, omegas_ref, out_ref):
    def lookup(index, table):
        high, low = index // 128, index % 128
        block = lax.broadcasted_iota(jnp.int32, (table.shape[0], PAIRS), 0)
        picked = lax.dot_general(
            table,
            (block == high).astype(jnp.float32),
            (((0,), (0,)), ((), ())),
            precision=lax.Precision.HIGHEST,
            preferred_element_type=jnp.float32,
        )
        lane = lax.broadcasted_iota(jnp.int32, (128, PAIRS), 0)
        return jnp.sum(jnp.where(lane == low, picked, 0.0), axis=0, keepdims=True)

    gap = lookup(conduction_ref[...], cond_ref[...]) - lookup(valence_ref[...], val_ref[...])
    for f in range(2):
        omega = omegas_ref[f]
        out_ref[f : f + 1, :] = -4.0 * gap / (gap * gap + omega * omega)


VMEM = pl.BlockSpec(memory_space=pltpu.VMEM)
SMEM = pl.BlockSpec(memory_space=pltpu.SMEM)


def pair_weights(valence_index, conduction_index, val_energy, cond_energy, omegas):
    def order(index):
        return index.reshape(GROUP, 2, GROUP, OWN).transpose(2, 0, 1, 3).reshape(1, PAIRS)

    return pl.pallas_call(
        weights_kernel,
        out_shape=jax.ShapeDtypeStruct((2, PAIRS), jnp.float32),
        in_specs=[VMEM] * 4 + [SMEM],
        out_specs=VMEM,
        compiler_params=pltpu.CompilerParams(vmem_limit_bytes=24 << 20),
        name="weights",
    )(order(valence_index), order(conduction_index), spread(val_energy), spread(cond_energy), omegas)


def slices_kernel(core_ref, own_ref, other_ref, out_ref):
    core = core_ref[0]
    for s in range(GROUP):
        lanes = slice(s * COLUMNS, (s + 1) * COLUMNS)
        out_ref[s, core, :, :COLUMNS] = own_ref[:, lanes]
        out_ref[s, 1 - core, :, :COLUMNS] = other_ref[:, lanes]
    out_ref[:, :, :, COLUMNS:] = jnp.zeros((GROUP, 2, OWN, PADDED - COLUMNS), jnp.bfloat16)


def slices(core, own, other):
    return pl.pallas_call(
        slices_kernel,
        out_shape=jax.ShapeDtypeStruct((GROUP, 2, OWN, PADDED), jnp.bfloat16),
        in_specs=[SMEM, VMEM, VMEM],
        out_specs=VMEM,
        compiler_params=pltpu.CompilerParams(vmem_limit_bytes=16 << 20),
        name="slices",
    )(core, own, other)


def turn_kernel(core_ref, in_ref, out_ref):
    @pl.when(core_ref[0] == 0)
    def _():
        for half in range(2):
            part = in_ref[:, half * ROWS : (half + 1) * ROWS]
            part = jnp.concatenate([part, jnp.zeros((BLOCK, HALF - ROWS), jnp.bfloat16)], axis=1)
            out_ref[half * HALF : (half + 1) * HALF, :] = part.T

    @pl.when(core_ref[0] == 1)
    def _():
        for p in range(PANELS):
            out_ref[p * BLOCK : (p + 1) * BLOCK, :] = in_ref[:, p * PANEL : (p + 1) * PANEL]


def turn(core, value):
    return pl.pallas_call(
        turn_kernel,
        out_shape=jax.ShapeDtypeStruct((PADDED, BLOCK), jnp.bfloat16),
        in_specs=[SMEM, VMEM],
        out_specs=VMEM,
        compiler_params=pltpu.CompilerParams(vmem_limit_bytes=16 << 20),
        name="turn",
    )(core, value)


def product_kernel(place_ref, weight_ref, *refs):
    mine, theirs = refs[:GROUP], refs[GROUP : 2 * GROUP]
    out_ref, rows, scaled, columns, rows_sem, columns_sem = refs[2 * GROUP :]
    j = pl.program_id(0)
    core = place_ref[0]

    def row_copy(k, refs):
        half = refs[k].at[pl.ds(pl.multiple_of(core * HALF, HALF), HALF)]
        return pltpu.make_async_copy(half, rows.at[place_ref[1 + k]], rows_sem.at[k])

    def column_copy(k, refs):
        block = refs[k].reshape(PANELS, GROUP, 2 * OWN, PANEL)
        return pltpu.make_async_copy(block, columns.at[:, :, place_ref[1 + GROUP + k]], columns_sem.at[k])

    @pl.when(j == 0)
    def _():
        for which, first, second in ((0, mine, theirs), (1, theirs, mine)):

            @pl.when(core == which)
            def _(first=first, second=second):
                for k in range(GROUP):
                    row_copy(k, first).start()
                for k in range(GROUP):
                    column_copy(k, second).start()

        for k in range(GROUP):
            row_copy(k, mine).wait()
        for n in range(GROUP):
            part = rows[n, :ROWS].astype(jnp.float32)
            lanes = slice(n * BLOCK, (n + 1) * BLOCK)
            for f in range(2):
                scaled[f, :, lanes] = (part * weight_ref[f : f + 1, lanes]).astype(jnp.bfloat16)
        for k in range(GROUP):
            column_copy(k, mine).wait()

    right = columns[j].reshape(PAIRS, PANEL)
    for f in range(2):
        out_ref[f] = jnp.dot(scaled[f], right, preferred_element_type=jnp.float32)


def product(place, weight, mine, theirs):
    any_space = pl.BlockSpec(memory_space=pl.ANY)
    return pl.pallas_call(
        product_kernel,
        grid=(PANELS,),
        out_shape=jax.ShapeDtypeStruct((2, ROWS, COLUMNS), jnp.float32),
        in_specs=[SMEM, VMEM] + [any_space] * (2 * GROUP),
        out_specs=pl.BlockSpec((2, ROWS, PANEL), lambda j: (0, 0, j)),
        scratch_shapes=[
            pltpu.VMEM((GROUP, HALF, BLOCK), jnp.bfloat16),
            pltpu.VMEM((2, ROWS, PAIRS), jnp.bfloat16),
            pltpu.VMEM((PANELS, GROUP, GROUP, 2 * OWN, PANEL), jnp.bfloat16),
            pltpu.SemaphoreType.DMA((GROUP,)),
            pltpu.SemaphoreType.DMA((GROUP,)),
        ],
        compiler_params=pltpu.CompilerParams(vmem_limit_bytes=40 << 20),
        cost_estimate=pl.CostEstimate(
            flops=4 * ROWS * COLUMNS * PAIRS, bytes_accessed=28 << 20, transcendentals=0
        ),
        name="product",
    )(place, weight, *mine, *theirs)


def exchange(value):
    wide = [[device(a // 4, a % 4, 0, xl, y) for a in range(GROUP)] for xl in range(2) for y in range(4)]
    narrow = [[device(xh, z, 1, b // 4, b % 4) for b in range(GROUP)] for xh in range(2) for z in range(4)]
    return lax.all_to_all(value, ALL, 0, 0, axis_index_groups=wide + narrow, tiled=True)


def gather(own):
    beside = swap_x(own)
    near = [own, beside]
    up = [ring(v, 1) for v in near]
    down = [ring(v, -1) for v in near]
    far = [ring(up[0], 1), ring(down[1], -1)]
    return near + up + down + far


def places(core):
    def of(x, around):
        shifts = (0, 0, 3, 3, 1, 1, 2, 2)
        return [(x + k) % 2 * 4 + (around + shift) % 4 for k, shift in enumerate(shifts)]

    rows = of(lax.axis_index("xl"), lax.axis_index("y"))
    columns = of(lax.axis_index("xh"), lax.axis_index("z"))
    return jnp.stack([core] + rows + columns).astype(jnp.int32)


def body(pair_elements, valence_index, conduction_index, val_energy, cond_energy, omegas):
    core = lax.axis_index("c").astype(jnp.int32)
    weight = pair_weights(valence_index, conduction_index, val_energy, cond_energy, omegas)
    part = exchange(slices(core[None], pair_elements, swap_cores(pair_elements)))
    mine = gather(turn(core[None], part.reshape(BLOCK, PADDED)))
    theirs = [swap_cores(v) for v in mine]
    return product(places(core), weight, mine, theirs)


def solution(mesh):
    fine = Mesh(mesh.devices.reshape(SIZES), ALL)
    wide, narrow = ("xh", "z", "c"), ("xl", "y")
    return jax.shard_map(
        body,
        mesh=fine,
        in_specs=(P(wide + narrow, None), P(), P(), P(), P(), P()),
        out_specs=P(None, wide, narrow),
        check_vma=False,
    )
```

```python
import jax
import jax.numpy as jnp
from jax import lax
from jax.experimental import pallas as pl
from jax.experimental.pallas import tpu as pltpu
from jax.sharding import Mesh, PartitionSpec as P

ALL = ("xh", "z", "c", "xl", "y")
SIZES = (2, 4, 2, 2, 4)
ROWS = 1000
COLUMNS = 2000
GROUP = 8
OWN = 16
PAIRS = GROUP * GROUP * 2 * OWN
BLOCK = GROUP * 2 * OWN
PADDED = 2048
PANEL = 256
PANELS = PADDED // PANEL
HALF = 1024
WIDTH = 2
STEPS = PANELS // WIDTH


def device(xh, z, c, xl, y):
    return (((xh % 2 * 4 + z % 4) * 2 + c) * 2 + xl % 2) * 4 + y % 4


def every():
    return [(xh, z, c, xl, y) for xh in range(2) for z in range(4) for c in range(2) for xl in range(2) for y in range(4)]


def move(value, to):
    return lax.ppermute(value, ALL, [(device(*d), device(*to(*d))) for d in every()])


def swap_cores(value):
    return move(value, lambda xh, z, c, xl, y: (xh, z, 1 - c, xl, y))


def swap_x(value):
    return move(value, lambda xh, z, c, xl, y: (xh, z, c, xl + 1, y) if c == 0 else (xh + 1, z, c, xl, y))


def ring(value, by):
    return move(value, lambda xh, z, c, xl, y: (xh, z, c, xl, y + by) if c == 0 else (xh, z + by, c, xl, y))


def spread(table):
    rows = -(-table.shape[0] // 1024) * 8
    return jnp.pad(table, (0, rows * 128 - table.shape[0])).reshape(rows, 128)


def weights_kernel(valence_ref, conduction_ref, val_ref, cond_ref, omegas_ref, out_ref):
    def lookup(index, table):
        high, low = index // 128, index % 128
        block = lax.broadcasted_iota(jnp.int32, (table.shape[0], PAIRS), 0)
        picked = lax.dot_general(
            table,
            (block == high).astype(jnp.float32),
            (((0,), (0,)), ((), ())),
            precision=lax.Precision.HIGHEST,
            preferred_element_type=jnp.float32,
        )
        lane = lax.broadcasted_iota(jnp.int32, (128, PAIRS), 0)
        return jnp.sum(jnp.where(lane == low, picked, 0.0), axis=0, keepdims=True)

    gap = lookup(conduction_ref[...], cond_ref[...]) - lookup(valence_ref[...], val_ref[...])
    for f in range(2):
        omega = omegas_ref[f]
        out_ref[f : f + 1, :] = -4.0 * gap / (gap * gap + omega * omega)


VMEM = pl.BlockSpec(memory_space=pltpu.VMEM)
SMEM = pl.BlockSpec(memory_space=pltpu.SMEM)


def pair_weights(valence_index, conduction_index, val_energy, cond_energy, omegas):
    def order(index):
        return index.reshape(GROUP, 2, GROUP, OWN).transpose(2, 0, 1, 3).reshape(1, PAIRS)

    return pl.pallas_call(
        weights_kernel,
        out_shape=jax.ShapeDtypeStruct((2, PAIRS), jnp.float32),
        in_specs=[VMEM] * 4 + [SMEM],
        out_specs=VMEM,
        compiler_params=pltpu.CompilerParams(vmem_limit_bytes=24 << 20),
        name="weights",
    )(order(valence_index), order(conduction_index), spread(val_energy), spread(cond_energy), omegas)


def slices_kernel(core_ref, own_ref, other_ref, out_ref):
    core = core_ref[0]
    for s in range(GROUP):
        lanes = slice(s * COLUMNS, (s + 1) * COLUMNS)
        out_ref[s, core, :, :COLUMNS] = own_ref[:, lanes]
        out_ref[s, 1 - core, :, :COLUMNS] = other_ref[:, lanes]
    out_ref[:, :, :, COLUMNS:] = jnp.zeros((GROUP, 2, OWN, PADDED - COLUMNS), jnp.bfloat16)


def slices(core, own, other):
    return pl.pallas_call(
        slices_kernel,
        out_shape=jax.ShapeDtypeStruct((GROUP, 2, OWN, PADDED), jnp.bfloat16),
        in_specs=[SMEM, VMEM, VMEM],
        out_specs=VMEM,
        compiler_params=pltpu.CompilerParams(vmem_limit_bytes=16 << 20),
        name="slices",
    )(core, own, other)


def turn_kernel(core_ref, in_ref, out_ref):
    @pl.when(core_ref[0] == 0)
    def _():
        for half in range(2):
            part = in_ref[:, half * ROWS : (half + 1) * ROWS]
            part = jnp.concatenate([part, jnp.zeros((BLOCK, HALF - ROWS), jnp.bfloat16)], axis=1)
            out_ref[half * HALF : (half + 1) * HALF, :] = part.T

    @pl.when(core_ref[0] == 1)
    def _():
        for p in range(PANELS):
            out_ref[p * BLOCK : (p + 1) * BLOCK, :] = in_ref[:, p * PANEL : (p + 1) * PANEL]


def turn(core, value):
    return pl.pallas_call(
        turn_kernel,
        out_shape=jax.ShapeDtypeStruct((PADDED, BLOCK), jnp.bfloat16),
        in_specs=[SMEM, VMEM],
        out_specs=VMEM,
        compiler_params=pltpu.CompilerParams(vmem_limit_bytes=16 << 20),
        name="turn",
    )(core, value)


RING = (0, 3, 1, 2)


def half_of(refs, k, which):
    if k == GROUP - 1:
        return refs[k + which]
    return refs[k].at[pl.ds(which * HALF, HALF)]


def product_kernel(place_ref, weight_ref, *refs):
    mine, theirs = refs[: GROUP + 1], refs[GROUP + 1 : 2 * GROUP + 2]
    out_ref, rows, scaled, columns, rows_sem, columns_sem = refs[2 * GROUP + 2 :]
    j = pl.program_id(0)
    core = place_ref[0]

    def row_copy(k, which, refs):
        return pltpu.make_async_copy(half_of(refs, k, which), rows.at[place_ref[1 + k]], rows_sem.at[k])

    def column_copy(k, step, refs):
        which, part = divmod(step, STEPS // 2)
        half = half_of(refs, k, which).at[pl.ds(part * WIDTH * BLOCK, WIDTH * BLOCK)]
        to = columns.at[pl.ds(step * WIDTH, WIDTH), :, place_ref[1 + GROUP + k]]
        return pltpu.make_async_copy(half.reshape(WIDTH, GROUP, 2 * OWN, PANEL), to, columns_sem.at[step, k])

    @pl.when(j == 0)
    def _():
        for which, first, second in ((0, mine, theirs), (1, theirs, mine)):

            @pl.when(core == which)
            def _(which=which, first=first, second=second):
                for k in range(GROUP):
                    row_copy(k, which, first).start()
                for k in range(GROUP):
                    column_copy(k, 0, second).start()

        for k in range(GROUP):
            row_copy(k, 0, mine).wait()

        for which, second in ((0, theirs), (1, mine)):

            @pl.when(core == which)
            def _(second=second):
                for step in range(1, STEPS):
                    for k in range(GROUP):
                        column_copy(k, step, second).start()

        for n in range(GROUP):
            part = rows[n, :ROWS].astype(jnp.float32)
            lanes = slice(n * BLOCK, (n + 1) * BLOCK)
            for f in range(2):
                scaled[f, :, lanes] = (part * weight_ref[f : f + 1, lanes]).astype(jnp.bfloat16)

    for step in range(STEPS):

        @pl.when(j == step)
        def _(step=step):
            for k in range(GROUP):
                column_copy(k, step, mine).wait()

    for panel in range(WIDTH):
        right = columns[j * WIDTH + panel].reshape(PAIRS, PANEL)
        for f in range(2):
            out_ref[f, :, panel * PANEL : (panel + 1) * PANEL] = jnp.dot(
                scaled[f], right, preferred_element_type=jnp.float32
            )


def product(place, weight, mine, theirs):
    return pl.pallas_call(
        product_kernel,
        grid=(STEPS,),
        out_shape=jax.ShapeDtypeStruct((2, ROWS, COLUMNS), jnp.float32),
        in_specs=[SMEM, VMEM] + [pl.BlockSpec(memory_space=pl.ANY)] * (2 * GROUP + 2),
        out_specs=pl.BlockSpec((2, ROWS, WIDTH * PANEL), lambda j: (0, 0, j)),
        scratch_shapes=[
            pltpu.VMEM((GROUP, HALF, BLOCK), jnp.bfloat16),
            pltpu.VMEM((2, ROWS, PAIRS), jnp.bfloat16),
            pltpu.VMEM((PANELS, GROUP, GROUP, 2 * OWN, PANEL), jnp.bfloat16),
            pltpu.SemaphoreType.DMA((GROUP,)),
            pltpu.SemaphoreType.DMA((STEPS, GROUP)),
        ],
        compiler_params=pltpu.CompilerParams(vmem_limit_bytes=32 << 20),
        cost_estimate=pl.CostEstimate(
            flops=4 * ROWS * COLUMNS * PAIRS, bytes_accessed=28 << 20, transcendentals=0
        ),
        name="product",
    )(place, weight, *mine, *theirs)


def exchange(value):
    wide = [[device(a // 4, a % 4, 0, xl, y) for a in range(GROUP)] for xl in range(2) for y in range(4)]
    narrow = [[device(xh, z, 1, b // 4, b % 4) for b in range(GROUP)] for xh in range(2) for z in range(4)]
    return lax.all_to_all(value, ALL, 0, 0, axis_index_groups=wide + narrow, tiled=True)


def gather(own, weight, place):
    near = [ring(own, by) for by in (1, -1, 2)]
    beside = swap_x(own)
    near, beside, weight, place = lax.optimization_barrier((near, beside, weight, place))
    late = [ring(beside, by) for by in (1, -1)]
    far = [swap_x(near[2][:HALF]), ring(beside[HALF:], 2)]
    mine = [own] + near + [beside] + late + far
    return mine, [swap_cores(v) for v in mine], weight, place


def places(core):
    def of(x, around):
        return [(x + k) % 2 * 4 + (around + shift) % 4 for k in range(2) for shift in RING]

    rows = of(lax.axis_index("xl"), lax.axis_index("y"))
    columns = of(lax.axis_index("xh"), lax.axis_index("z"))
    return jnp.stack([core] + rows + columns).astype(jnp.int32)


def body(pair_elements, valence_index, conduction_index, val_energy, cond_energy, omegas):
    core = lax.axis_index("c").astype(jnp.int32)
    weight = pair_weights(valence_index, conduction_index, val_energy, cond_energy, omegas)
    part = exchange(slices(core[None], pair_elements, swap_cores(pair_elements)))
    mine, theirs, weight, place = gather(turn(core[None], part.reshape(BLOCK, PADDED)), weight, places(core))
    return product(place, weight, mine, theirs)


def solution(mesh):
    fine = Mesh(mesh.devices.reshape(SIZES), ALL)
    wide, narrow = ("xh", "z", "c"), ("xl", "y")
    return jax.shard_map(
        body,
        mesh=fine,
        in_specs=(P(wide + narrow, None), P(), P(), P(), P(), P()),
        out_specs=P(None, wide, narrow),
        check_vma=False,
    )
```

```python
import jax
import jax.numpy as jnp
from jax import lax
from jax.experimental import pallas as pl
from jax.experimental.pallas import tpu as pltpu
from jax.sharding import Mesh, PartitionSpec as P

ALL = ("xh", "z", "c", "xl", "y")
SIZES = (2, 4, 2, 2, 4)
ROWS = 1000
COLUMNS = 2000
GROUP = 8
OWN = 16
PAIRS = GROUP * GROUP * 2 * OWN
BLOCK = GROUP * 2 * OWN
PADDED = 2048
PANEL = 256
PANELS = PADDED // PANEL
HALF = 1024
WIDTH = 2
STEPS = PANELS // WIDTH


def device(xh, z, c, xl, y):
    return (((xh % 2 * 4 + z % 4) * 2 + c) * 2 + xl % 2) * 4 + y % 4


def every():
    return [(xh, z, c, xl, y) for xh in range(2) for z in range(4) for c in range(2) for xl in range(2) for y in range(4)]


def move(value, to):
    return lax.ppermute(value, ALL, [(device(*d), device(*to(*d))) for d in every()])


def swap_cores(value):
    return move(value, lambda xh, z, c, xl, y: (xh, z, 1 - c, xl, y))


def swap_x(value):
    return move(value, lambda xh, z, c, xl, y: (xh, z, c, xl + 1, y) if c == 0 else (xh + 1, z, c, xl, y))


def ring(value, by):
    return move(value, lambda xh, z, c, xl, y: (xh, z, c, xl, y + by) if c == 0 else (xh, z + by, c, xl, y))


def spread(table):
    rows = -(-table.shape[0] // 1024) * 8
    return jnp.pad(table, (0, rows * 128 - table.shape[0])).reshape(rows, 128)


def weights_kernel(valence_ref, conduction_ref, val_ref, cond_ref, omegas_ref, out_ref):
    def lookup(index, table):
        high, low = index // 128, index % 128
        block = lax.broadcasted_iota(jnp.int32, (table.shape[0], PAIRS), 0)
        picked = lax.dot_general(
            table,
            (block == high).astype(jnp.float32),
            (((0,), (0,)), ((), ())),
            precision=lax.Precision.HIGHEST,
            preferred_element_type=jnp.float32,
        )
        lane = lax.broadcasted_iota(jnp.int32, (128, PAIRS), 0)
        return jnp.sum(jnp.where(lane == low, picked, 0.0), axis=0, keepdims=True)

    gap = lookup(conduction_ref[...], cond_ref[...]) - lookup(valence_ref[...], val_ref[...])
    for f in range(2):
        omega = omegas_ref[f]
        out_ref[f : f + 1, :] = -4.0 * gap / (gap * gap + omega * omega)


VMEM = pl.BlockSpec(memory_space=pltpu.VMEM)
ANY = pl.BlockSpec(memory_space=pl.ANY)
SMEM = pl.BlockSpec(memory_space=pltpu.SMEM)


def pair_weights(valence_index, conduction_index, val_energy, cond_energy, omegas):
    def order(index):
        return index.reshape(GROUP, 2, GROUP, OWN).transpose(2, 0, 1, 3).reshape(1, PAIRS)

    return pl.pallas_call(
        weights_kernel,
        out_shape=jax.ShapeDtypeStruct((2, PAIRS), jnp.float32),
        in_specs=[VMEM] * 4 + [SMEM],
        out_specs=VMEM,
        compiler_params=pltpu.CompilerParams(vmem_limit_bytes=24 << 20),
        name="weights",
    )(order(valence_index), order(conduction_index), spread(val_energy), spread(cond_energy), omegas)


def slices_kernel(which_ref, in_ref, *refs):
    out_ref = refs[-1]
    which = which_ref[0]
    for s in range(GROUP):
        out_ref[s, which, :, :COLUMNS] = in_ref[:, s * COLUMNS : (s + 1) * COLUMNS]
    out_ref[:, which, :, COLUMNS:] = jnp.zeros((GROUP, OWN, PADDED - COLUMNS), jnp.bfloat16)


def slices(which, pairs, *part):
    return pl.pallas_call(
        slices_kernel,
        out_shape=jax.ShapeDtypeStruct((GROUP, 2, OWN, PADDED), jnp.bfloat16),
        in_specs=[SMEM, VMEM] + [VMEM] * len(part),
        out_specs=VMEM,
        input_output_aliases={2: 0} if part else {},
        compiler_params=pltpu.CompilerParams(vmem_limit_bytes=16 << 20),
        name="slices",
    )(which, pairs, *part)


def turn_kernel(core_ref, in_ref, out_ref):
    @pl.when(core_ref[0] == 0)
    def _():
        for half in range(2):
            part = in_ref[:, half * ROWS : (half + 1) * ROWS]
            part = jnp.concatenate([part, jnp.zeros((BLOCK, HALF - ROWS), jnp.bfloat16)], axis=1)
            out_ref[half * HALF : (half + 1) * HALF, :] = part.T

    @pl.when(core_ref[0] == 1)
    def _():
        for p in range(PANELS):
            out_ref[p * BLOCK : (p + 1) * BLOCK, :] = in_ref[:, p * PANEL : (p + 1) * PANEL]


def turn(core, value):
    return pl.pallas_call(
        turn_kernel,
        out_shape=jax.ShapeDtypeStruct((PADDED, BLOCK), jnp.bfloat16),
        in_specs=[SMEM, VMEM],
        out_specs=VMEM,
        compiler_params=pltpu.CompilerParams(vmem_limit_bytes=16 << 20),
        name="turn",
    )(core, value)


RING = (0, 3, 1, 2)
NEAR = len(RING)
LANES = NEAR * 2 * OWN
NEAR_PAIRS = NEAR * LANES
LATE_PAIRS = PAIRS - NEAR_PAIRS


class Meta:
    def __init__(self, ref):
        self.core, self.xl, self.xh = ref[0], ref[1], ref[2]
        self.row = [ref[3 + k] for k in range(NEAR)]
        self.column = [ref[3 + NEAR + k] for k in range(NEAR)]


def half_of(refs, k, which):
    if k == GROUP - 1:
        return refs[k + which]
    return refs[k].at[pl.ds(which * HALF, HALF)]


def column_part(refs, k, step, x):
    which, part = divmod(step, STEPS // 2)
    ref = half_of(refs, k, which).at[pl.ds(part * WIDTH * BLOCK, WIDTH * BLOCK)]
    return ref.reshape(WIDTH, GROUP, 2 * OWN, PANEL).at[:, pl.ds(x * NEAR, NEAR)]


def panels(step):
    return pl.ds(step * WIDTH, WIDTH)


def by_core(meta, mine, theirs, run):
    @pl.when(meta.core == 0)
    def _():
        run(mine, theirs, 0)

    @pl.when(meta.core == 1)
    def _():
        run(theirs, mine, 1)


def scale(rows, y, x_row, x_column, weight_ref):
    lanes = pl.ds(pl.multiple_of(x_column * LANES, LANES), LANES)
    part = rows[y, :ROWS, lanes].astype(jnp.float32)
    start = pl.multiple_of((x_row * NEAR + y) * BLOCK + x_column * LANES, LANES)
    return [(part * weight_ref[f : f + 1, pl.ds(start, LANES)]).astype(jnp.bfloat16) for f in range(2)]


def early_kernel(meta_ref, weight_ref, *refs):
    mine, theirs = refs[:NEAR], refs[NEAR : 2 * NEAR]
    out_ref, next_ref, rows, scaled, columns, rows_sem, columns_sem = refs[2 * NEAR :]
    j = pl.program_id(0)
    meta = Meta(meta_ref)

    def row_copy(k, refs, core):
        return pltpu.make_async_copy(half_of(refs, k, core), rows.at[meta.row[k]], rows_sem.at[k])

    def column_copy(k, step, refs):
        to = columns.at[panels(step), :, meta.column[k]]
        return pltpu.make_async_copy(column_part(refs, k, step, meta.xl), to, columns_sem.at[step, k])

    @pl.when(j == 0)
    def _():
        def start(row_refs, column_refs, core):
            for k in range(NEAR):
                row_copy(k, row_refs, core).start()
            for step in range(STEPS):
                for k in range(NEAR):
                    column_copy(k, step, column_refs).start()

        by_core(meta, mine, theirs, start)
        for k in range(NEAR):
            row_copy(k, mine, 0).wait()
        for y in range(NEAR):
            lanes = slice(y * LANES, (y + 1) * LANES)
            for f, value in enumerate(scale(rows, y, meta.xl, meta.xh, weight_ref)):
                scaled[f, :, lanes] = value
            for f, value in enumerate(scale(rows, y, meta.xl, 1 - meta.xh, weight_ref)):
                next_ref[f, :, lanes] = value

    for step in range(STEPS):

        @pl.when(j == step)
        def _(step=step):
            for k in range(NEAR):
                column_copy(k, step, mine).wait()

    for panel in range(WIDTH):
        right = columns[j * WIDTH + panel].reshape(NEAR_PAIRS, PANEL)
        for f in range(2):
            out_ref[panel, f] = jnp.dot(scaled[f], right, preferred_element_type=jnp.float32)


def cost(pairs, size):
    return pl.CostEstimate(flops=4 * ROWS * COLUMNS * pairs, bytes_accessed=size, transcendentals=0)


def early_product(meta, weight, mine, theirs):
    return pl.pallas_call(
        early_kernel,
        grid=(STEPS,),
        out_shape=(
            pltpu.HBM((PANELS, 2, ROWS, PANEL), jnp.float32),
            jax.ShapeDtypeStruct((2, ROWS, NEAR_PAIRS), jnp.bfloat16),
        ),
        in_specs=[SMEM, VMEM] + [ANY] * (2 * NEAR),
        out_specs=(
            pl.BlockSpec((WIDTH, 2, ROWS, PANEL), lambda j: (j, 0, 0, 0)),
            pl.BlockSpec((2, ROWS, NEAR_PAIRS), lambda j: (0, 0, 0)),
        ),
        scratch_shapes=[
            pltpu.VMEM((NEAR, HALF, BLOCK), jnp.bfloat16),
            pltpu.VMEM((2, ROWS, NEAR_PAIRS), jnp.bfloat16),
            pltpu.VMEM((PANELS, NEAR, NEAR, 2 * OWN, PANEL), jnp.bfloat16),
            pltpu.SemaphoreType.DMA((NEAR,)),
            pltpu.SemaphoreType.DMA((STEPS, NEAR)),
        ],
        compiler_params=pltpu.CompilerParams(vmem_limit_bytes=24 << 20),
        name="early_product",
    )(meta, weight, *mine, *theirs)


def late_kernel(meta_ref, weight_ref, sum_ref, next_ref, *refs):
    count = GROUP + 1
    mine, theirs = refs[:count], refs[count : 2 * count]
    out_ref, rows, scaled, columns, sums, rows_sem, columns_sem, sums_sem, next_sem = refs[2 * count :]
    j = pl.program_id(0)
    meta = Meta(meta_ref)

    def row_copy(k, refs, core):
        return pltpu.make_async_copy(half_of(refs, NEAR + k, core), rows.at[meta.row[k]], rows_sem.at[k])

    def column_copies(step, refs):
        copies = []
        for k in range(GROUP):
            beside, place = k // NEAR, meta.column[k % NEAR]
            to = columns.at[panels(step), pl.ds((1 + beside) * NEAR, NEAR), place]
            part = column_part(refs, k, step, 1 - meta.xl)
            copies.append(pltpu.make_async_copy(part, to, columns_sem.at[step, k]))
            if beside:
                to = columns.at[panels(step), pl.ds(0, NEAR), place]
                part = column_part(refs, k, step, meta.xl)
                copies.append(pltpu.make_async_copy(part, to, columns_sem.at[step, NEAR + k]))
        return copies

    def sum_copy(step):
        return pltpu.make_async_copy(sum_ref.at[panels(step)], sums, sums_sem)

    next_copy = pltpu.make_async_copy(next_ref, scaled.at[:, :, pl.ds(0, NEAR_PAIRS)], next_sem)

    def step_dot(step, panel, f, pairs):
        right = columns[step * WIDTH + panel].reshape(LATE_PAIRS, PANEL)[pairs]
        return jnp.dot(scaled[f, :, pairs], right, preferred_element_type=jnp.float32)

    for step in range(STEPS):

        @pl.when(j == step)
        def _(step=step):
            if step == 0:

                def start_first(row_refs, column_refs, core):
                    for k in range(NEAR):
                        row_copy(k, row_refs, core).start()
                    next_copy.start()
                    for copy in column_copies(0, column_refs):
                        copy.start()

                def start_rest(row_refs, column_refs, core):
                    for step in range(1, STEPS):
                        for copy in column_copies(step, column_refs):
                            copy.start()

                by_core(meta, mine, theirs, start_first)
                for k in range(NEAR):
                    row_copy(k, mine, 0).wait()
                next_copy.wait()
                sum_copy(0).start()
                by_core(meta, mine, theirs, start_rest)
            for copy in column_copies(step, mine):
                copy.wait()
            lanes = [slice(panel * PANEL, (panel + 1) * PANEL) for panel in range(WIDTH)]
            if step == 0:
                for panel in range(WIDTH):
                    for f in range(2):
                        out_ref[f, :, lanes[panel]] = step_dot(0, panel, f, slice(0, NEAR_PAIRS))
                for y in range(NEAR):
                    for beside in range(2):
                        first = ((1 + beside) * NEAR + y) * LANES
                        x_column = meta.xh if beside == 0 else 1 - meta.xh
                        for f, value in enumerate(scale(rows, y, 1 - meta.xl, x_column, weight_ref)):
                            scaled[f, :, first : first + LANES] = value
            sum_copy(step).wait()
            for panel in range(WIDTH):
                for f in range(2):
                    total = sums[panel, f]
                    if step == 0:
                        total = total + out_ref[f, :, lanes[panel]]
                    pairs = slice(NEAR_PAIRS if step == 0 else 0, LATE_PAIRS)
                    out_ref[f, :, lanes[panel]] = total + step_dot(step, panel, f, pairs)
            if step + 1 < STEPS:
                sum_copy(step + 1).start()


def late_product(meta, weight, total, following, mine, theirs):
    return pl.pallas_call(
        late_kernel,
        grid=(STEPS,),
        out_shape=jax.ShapeDtypeStruct((2, ROWS, COLUMNS), jnp.float32),
        in_specs=[SMEM, VMEM] + [ANY] * (2 * GROUP + 4),
        out_specs=pl.BlockSpec((2, ROWS, WIDTH * PANEL), lambda j: (0, 0, j)),
        scratch_shapes=[
            pltpu.VMEM((NEAR, HALF, BLOCK), jnp.bfloat16),
            pltpu.VMEM((2, ROWS, LATE_PAIRS), jnp.bfloat16),
            pltpu.VMEM((PANELS, 3 * NEAR, NEAR, 2 * OWN, PANEL), jnp.bfloat16),
            pltpu.VMEM((WIDTH, 2, ROWS, PANEL), jnp.float32),
            pltpu.SemaphoreType.DMA((NEAR,)),
            pltpu.SemaphoreType.DMA((STEPS, GROUP + NEAR)),
            pltpu.SemaphoreType.DMA,
            pltpu.SemaphoreType.DMA,
        ],
        compiler_params=pltpu.CompilerParams(vmem_limit_bytes=32 << 20),
        cost_estimate=cost(LATE_PAIRS, 48 << 20),
        name="late_product",
    )(meta, weight, total, following, *mine, *theirs)


def exchange(value):
    wide = [[device(a // 4, a % 4, 0, xl, y) for a in range(GROUP)] for xl in range(2) for y in range(4)]
    narrow = [[device(xh, z, 1, b // 4, b % 4) for b in range(GROUP)] for xh in range(2) for z in range(4)]
    return lax.all_to_all(value, ALL, 0, 0, axis_index_groups=wide + narrow, tiled=True)


def describe():
    def around(axis):
        return [(lax.axis_index(axis) + shift) % NEAR for shift in RING]

    own = [lax.axis_index(axis) for axis in ("c", "xl", "xh")]
    return jnp.stack(own + around("y") + around("z")).astype(jnp.int32)


def body(pair_elements, valence_index, conduction_index, val_energy, cond_energy, omegas):
    core = lax.axis_index("c").astype(jnp.int32)[None]
    meta = describe()
    part = slices(1 - core, swap_cores(pair_elements), slices(core, pair_elements))
    part = exchange(part)
    own = turn(core, part.reshape(BLOCK, PADDED))
    weight = pair_weights(valence_index, conduction_index, val_energy, cond_energy, omegas)
    near = [ring(own, by) for by in (1, -1, 2)]
    beside = swap_x(own)
    near, beside, weight, meta = lax.optimization_barrier((near, beside, weight, meta))
    late = [ring(beside, by) for by in (1, -1)]
    far = [swap_x(near[2][:HALF]), ring(beside[HALF:], 2)]
    mine = [own] + near
    theirs = [swap_cores(v) for v in mine]
    total, following = early_product(meta, weight, mine, theirs)
    beside, far, total = lax.optimization_barrier((beside, far, total))
    others = [swap_cores(v) for v in [beside] + far]
    late, others = lax.optimization_barrier((late, others))
    mine += [beside] + late + far
    theirs += [others[0]] + [swap_cores(v) for v in late] + others[1:]
    return late_product(meta, weight, total, following, mine, theirs)


def solution(mesh):
    fine = Mesh(mesh.devices.reshape(SIZES), ALL)
    wide, narrow = ("xh", "z", "c"), ("xl", "y")
    return jax.shard_map(
        body,
        mesh=fine,
        in_specs=(P(wide + narrow, None), P(), P(), P(), P(), P()),
        out_specs=P(None, wide, narrow),
        check_vma=False,
    )
```

```python
import jax
import jax.numpy as jnp
from jax import lax
from jax.experimental import pallas as pl
from jax.experimental.pallas import tpu as pltpu
from jax.sharding import Mesh, PartitionSpec as P

ALL = ("xh", "z", "c", "xl", "y")
SIZES = (2, 4, 2, 2, 4)
ROWS = 1000
COLUMNS = 2000
GROUP = 8
OWN = 16
PAIRS = GROUP * GROUP * 2 * OWN
BLOCK = GROUP * 2 * OWN
PADDED = 2048
PANEL = 256
PANELS = PADDED // PANEL
HALF = 1024
WIDTH = 2
STEPS = PANELS // WIDTH


def device(xh, z, c, xl, y):
    return (((xh % 2 * 4 + z % 4) * 2 + c) * 2 + xl % 2) * 4 + y % 4


def every():
    return [(xh, z, c, xl, y) for xh in range(2) for z in range(4) for c in range(2) for xl in range(2) for y in range(4)]


def move(value, to):
    return lax.ppermute(value, ALL, [(device(*d), device(*to(*d))) for d in every()])


def swap_cores(value):
    return move(value, lambda xh, z, c, xl, y: (xh, z, 1 - c, xl, y))


def swap_x(value):
    return move(value, lambda xh, z, c, xl, y: (xh, z, c, xl + 1, y) if c == 0 else (xh + 1, z, c, xl, y))


def ring(value, by):
    return move(value, lambda xh, z, c, xl, y: (xh, z, c, xl, y + by) if c == 0 else (xh, z + by, c, xl, y))


def spread(table):
    rows = -(-table.shape[0] // 1024) * 8
    return jnp.pad(table, (0, rows * 128 - table.shape[0])).reshape(rows, 128)


def weights_kernel(valence_ref, conduction_ref, val_ref, cond_ref, omegas_ref, out_ref):
    def lookup(index, table):
        high, low = index // 128, index % 128
        block = lax.broadcasted_iota(jnp.int32, (table.shape[0], PAIRS), 0)
        picked = lax.dot_general(
            table,
            (block == high).astype(jnp.float32),
            (((0,), (0,)), ((), ())),
            precision=lax.Precision.HIGHEST,
            preferred_element_type=jnp.float32,
        )
        lane = lax.broadcasted_iota(jnp.int32, (128, PAIRS), 0)
        return jnp.sum(jnp.where(lane == low, picked, 0.0), axis=0, keepdims=True)

    gap = lookup(conduction_ref[...], cond_ref[...]) - lookup(valence_ref[...], val_ref[...])
    for f in range(2):
        omega = omegas_ref[f]
        out_ref[f : f + 1, :] = -4.0 * gap / (gap * gap + omega * omega)


VMEM = pl.BlockSpec(memory_space=pltpu.VMEM)
ANY = pl.BlockSpec(memory_space=pl.ANY)
SMEM = pl.BlockSpec(memory_space=pltpu.SMEM)


def pair_weights(valence_index, conduction_index, val_energy, cond_energy, omegas):
    def order(index):
        return index.reshape(GROUP, 2, GROUP, OWN).transpose(2, 0, 1, 3).reshape(1, PAIRS)

    return pl.pallas_call(
        weights_kernel,
        out_shape=jax.ShapeDtypeStruct((2, PAIRS), jnp.float32),
        in_specs=[VMEM] * 4 + [SMEM],
        out_specs=VMEM,
        compiler_params=pltpu.CompilerParams(vmem_limit_bytes=24 << 20),
        name="weights",
    )(order(valence_index), order(conduction_index), spread(val_energy), spread(cond_energy), omegas)


def slices_kernel(which_ref, in_ref, *refs):
    out_ref = refs[-1]
    which = which_ref[0]
    for s in range(GROUP):
        out_ref[s, which, :, :COLUMNS] = in_ref[:, s * COLUMNS : (s + 1) * COLUMNS]
    out_ref[:, which, :, COLUMNS:] = jnp.zeros((GROUP, OWN, PADDED - COLUMNS), jnp.bfloat16)


def slices(which, pairs, *part):
    return pl.pallas_call(
        slices_kernel,
        out_shape=jax.ShapeDtypeStruct((GROUP, 2, OWN, PADDED), jnp.bfloat16),
        in_specs=[SMEM, VMEM] + [VMEM] * len(part),
        out_specs=VMEM,
        input_output_aliases={2: 0} if part else {},
        compiler_params=pltpu.CompilerParams(vmem_limit_bytes=16 << 20),
        name="slices",
    )(which, pairs, *part)


def turn_kernel(core_ref, in_ref, out_ref):
    @pl.when(core_ref[0] == 0)
    def _():
        for half in range(2):
            part = in_ref[:, half * ROWS : (half + 1) * ROWS]
            part = jnp.concatenate([part, jnp.zeros((BLOCK, HALF - ROWS), jnp.bfloat16)], axis=1)
            out_ref[half * HALF : (half + 1) * HALF, :] = part.T

    @pl.when(core_ref[0] == 1)
    def _():
        for p in range(PANELS):
            out_ref[p * BLOCK : (p + 1) * BLOCK, :] = in_ref[:, p * PANEL : (p + 1) * PANEL]


def turn(core, value):
    return pl.pallas_call(
        turn_kernel,
        out_shape=jax.ShapeDtypeStruct((PADDED, BLOCK), jnp.bfloat16),
        in_specs=[SMEM, VMEM],
        out_specs=VMEM,
        compiler_params=pltpu.CompilerParams(vmem_limit_bytes=16 << 20),
        name="turn",
    )(core, value)


RING = (0, 3, 1, 2)
NEAR = len(RING)
LANES = NEAR * 2 * OWN
NEAR_PAIRS = NEAR * LANES
LATE_PAIRS = PAIRS - NEAR_PAIRS


class Meta:
    def __init__(self, ref):
        self.core, self.xl, self.xh = ref[0], ref[1], ref[2]
        self.row = [ref[3 + k] for k in range(NEAR)]
        self.column = [ref[3 + NEAR + k] for k in range(NEAR)]


def half_of(refs, k, which):
    if k == GROUP - 1:
        return refs[k + which]
    return refs[k].at[pl.ds(which * HALF, HALF)]


def column_part(refs, k, step, x):
    which, part = divmod(step, STEPS // 2)
    ref = half_of(refs, k, which).at[pl.ds(part * WIDTH * BLOCK, WIDTH * BLOCK)]
    return ref.reshape(WIDTH, GROUP, 2 * OWN, PANEL).at[:, pl.ds(x * NEAR, NEAR)]


def panels(step):
    return pl.ds(step * WIDTH, WIDTH)


def by_core(meta, mine, theirs, run):
    @pl.when(meta.core == 0)
    def _():
        run(mine, theirs, 0)

    @pl.when(meta.core == 1)
    def _():
        run(theirs, mine, 1)


def scale(rows, y, x_row, x_column, weight_ref):
    lanes = pl.ds(pl.multiple_of(x_column * LANES, LANES), LANES)
    part = rows[y, :ROWS, lanes].astype(jnp.float32)
    start = pl.multiple_of((x_row * NEAR + y) * BLOCK + x_column * LANES, LANES)
    return [(part * weight_ref[f : f + 1, pl.ds(start, LANES)]).astype(jnp.bfloat16) for f in range(2)]


def early_kernel(meta_ref, weight_ref, *refs):
    mine, theirs = refs[:NEAR], refs[NEAR : 2 * NEAR]
    out_ref, next_ref, rows, scaled, columns, rows_sem, columns_sem = refs[2 * NEAR :]
    j = pl.program_id(0)
    meta = Meta(meta_ref)

    def row_copy(k, refs, core):
        return pltpu.make_async_copy(half_of(refs, k, core), rows.at[meta.row[k]], rows_sem.at[k])

    def column_copy(k, step, refs):
        to = columns.at[panels(step), :, meta.column[k]]
        return pltpu.make_async_copy(column_part(refs, k, step, meta.xl), to, columns_sem.at[step, k])

    @pl.when(j == 0)
    def _():
        def start(row_refs, column_refs, core):
            for k in range(NEAR):
                row_copy(k, row_refs, core).start()
            for step in range(STEPS):
                for k in range(NEAR):
                    column_copy(k, step, column_refs).start()

        by_core(meta, mine, theirs, start)
        for k in range(NEAR):
            row_copy(k, mine, 0).wait()
        for y in range(NEAR):
            lanes = slice(y * LANES, (y + 1) * LANES)
            for f, value in enumerate(scale(rows, y, meta.xl, meta.xh, weight_ref)):
                scaled[f, :, lanes] = value
            for f, value in enumerate(scale(rows, y, meta.xl, 1 - meta.xh, weight_ref)):
                next_ref[f, :, lanes] = value

    for step in range(STEPS):

        @pl.when(j == step)
        def _(step=step):
            for k in range(NEAR):
                column_copy(k, step, mine).wait()

    for panel in range(WIDTH):
        right = columns[j * WIDTH + panel].reshape(NEAR_PAIRS, PANEL)
        for f in range(2):
            out_ref[panel, f] = jnp.dot(scaled[f], right, preferred_element_type=jnp.float32)


def cost(pairs, size):
    return pl.CostEstimate(flops=4 * ROWS * COLUMNS * pairs, bytes_accessed=size, transcendentals=0)


def early_product(meta, weight, mine, theirs):
    return pl.pallas_call(
        early_kernel,
        grid=(STEPS,),
        out_shape=(
            pltpu.HBM((PANELS, 2, ROWS, PANEL), jnp.float32),
            jax.ShapeDtypeStruct((2, ROWS, NEAR_PAIRS), jnp.bfloat16),
        ),
        in_specs=[SMEM, VMEM] + [ANY] * (2 * NEAR),
        out_specs=(
            pl.BlockSpec((WIDTH, 2, ROWS, PANEL), lambda j: (j, 0, 0, 0)),
            pl.BlockSpec((2, ROWS, NEAR_PAIRS), lambda j: (0, 0, 0)),
        ),
        scratch_shapes=[
            pltpu.VMEM((NEAR, HALF, BLOCK), jnp.bfloat16),
            pltpu.VMEM((2, ROWS, NEAR_PAIRS), jnp.bfloat16),
            pltpu.VMEM((PANELS, NEAR, NEAR, 2 * OWN, PANEL), jnp.bfloat16),
            pltpu.SemaphoreType.DMA((NEAR,)),
            pltpu.SemaphoreType.DMA((STEPS, NEAR)),
        ],
        compiler_params=pltpu.CompilerParams(vmem_limit_bytes=24 << 20),
        name="early_product",
    )(meta, weight, *mine, *theirs)


def late_kernel(meta_ref, weight_ref, sum_ref, next_ref, *refs):
    count = GROUP + 1
    mine, theirs = refs[:count], refs[count : 2 * count]
    out_ref, rows, scaled, columns, sums, rows_sem, columns_sem, sums_sem, next_sem = refs[2 * count :]
    j = pl.program_id(0)
    meta = Meta(meta_ref)

    def row_copy(k, refs, core):
        return pltpu.make_async_copy(half_of(refs, NEAR + k, core), rows.at[meta.row[k]], rows_sem.at[k])

    def column_copies(step, refs):
        copies = []
        for k in range(GROUP):
            beside, place = k // NEAR, meta.column[k % NEAR]
            to = columns.at[panels(step), pl.ds((1 + beside) * NEAR, NEAR), place]
            part = column_part(refs, k, step, 1 - meta.xl)
            copies.append(pltpu.make_async_copy(part, to, columns_sem.at[step, k]))
            if beside:
                to = columns.at[panels(step), pl.ds(0, NEAR), place]
                part = column_part(refs, k, step, meta.xl)
                copies.append(pltpu.make_async_copy(part, to, columns_sem.at[step, NEAR + k]))
        return copies

    def sum_copy(step):
        return pltpu.make_async_copy(sum_ref.at[panels(step)], sums.at[step % 2], sums_sem.at[step % 2])

    next_copy = pltpu.make_async_copy(next_ref, scaled.at[:, :, pl.ds(0, NEAR_PAIRS)], next_sem)

    def step_dot(step, panel, f, pairs):
        right = columns[step * WIDTH + panel].reshape(LATE_PAIRS, PANEL)[pairs]
        return jnp.dot(scaled[f, :, pairs], right, preferred_element_type=jnp.float32)

    for step in range(STEPS):

        @pl.when(j == step)
        def _(step=step):
            if step == 0:

                def start_first(row_refs, column_refs, core):
                    for k in range(NEAR):
                        row_copy(k, row_refs, core).start()
                    next_copy.start()
                    for copy in column_copies(0, column_refs):
                        copy.start()

                def start_rest(row_refs, column_refs, core):
                    for step in range(1, STEPS):
                        for copy in column_copies(step, column_refs):
                            copy.start()

                by_core(meta, mine, theirs, start_first)
                for k in range(NEAR):
                    row_copy(k, mine, 0).wait()
                next_copy.wait()
                sum_copy(0).start()
                by_core(meta, mine, theirs, start_rest)
            for copy in column_copies(step, mine):
                copy.wait()
            if step + 1 < STEPS:
                sum_copy(step + 1).start()
            lanes = [slice(panel * PANEL, (panel + 1) * PANEL) for panel in range(WIDTH)]
            if step == 0:
                for panel in range(WIDTH):
                    for f in range(2):
                        out_ref[f, :, lanes[panel]] = step_dot(0, panel, f, slice(0, NEAR_PAIRS))
                for y in range(NEAR):
                    for beside in range(2):
                        first = ((1 + beside) * NEAR + y) * LANES
                        x_column = meta.xh if beside == 0 else 1 - meta.xh
                        for f, value in enumerate(scale(rows, y, 1 - meta.xl, x_column, weight_ref)):
                            scaled[f, :, first : first + LANES] = value
            sum_copy(step).wait()
            for panel in range(WIDTH):
                for f in range(2):
                    total = sums[step % 2, panel, f]
                    if step == 0:
                        total = total + out_ref[f, :, lanes[panel]]
                    pairs = slice(NEAR_PAIRS if step == 0 else 0, LATE_PAIRS)
                    out_ref[f, :, lanes[panel]] = total + step_dot(step, panel, f, pairs)


def late_product(meta, weight, total, following, mine, theirs):
    return pl.pallas_call(
        late_kernel,
        grid=(STEPS,),
        out_shape=jax.ShapeDtypeStruct((2, ROWS, COLUMNS), jnp.float32),
        in_specs=[SMEM, VMEM] + [ANY] * (2 * GROUP + 4),
        out_specs=pl.BlockSpec((2, ROWS, WIDTH * PANEL), lambda j: (0, 0, j)),
        scratch_shapes=[
            pltpu.VMEM((NEAR, HALF, BLOCK), jnp.bfloat16),
            pltpu.VMEM((2, ROWS, LATE_PAIRS), jnp.bfloat16),
            pltpu.VMEM((PANELS, 3 * NEAR, NEAR, 2 * OWN, PANEL), jnp.bfloat16),
            pltpu.VMEM((2, WIDTH, 2, ROWS, PANEL), jnp.float32),
            pltpu.SemaphoreType.DMA((NEAR,)),
            pltpu.SemaphoreType.DMA((STEPS, GROUP + NEAR)),
            pltpu.SemaphoreType.DMA((2,)),
            pltpu.SemaphoreType.DMA,
        ],
        compiler_params=pltpu.CompilerParams(vmem_limit_bytes=36 << 20),
        cost_estimate=cost(LATE_PAIRS, 48 << 20),
        name="late_product",
    )(meta, weight, total, following, *mine, *theirs)


def exchange(value):
    wide = [[device(a // 4, a % 4, 0, xl, y) for a in range(GROUP)] for xl in range(2) for y in range(4)]
    narrow = [[device(xh, z, 1, b // 4, b % 4) for b in range(GROUP)] for xh in range(2) for z in range(4)]
    return lax.all_to_all(value, ALL, 0, 0, axis_index_groups=wide + narrow, tiled=True)


def describe():
    def around(axis):
        return [(lax.axis_index(axis) + shift) % NEAR for shift in RING]

    own = [lax.axis_index(axis) for axis in ("c", "xl", "xh")]
    return jnp.stack(own + around("y") + around("z")).astype(jnp.int32)


def body(pair_elements, valence_index, conduction_index, val_energy, cond_energy, omegas):
    core = lax.axis_index("c").astype(jnp.int32)[None]
    meta = describe()
    part = slices(1 - core, swap_cores(pair_elements), slices(core, pair_elements))
    part = exchange(part)
    own = turn(core, part.reshape(BLOCK, PADDED))
    weight = pair_weights(valence_index, conduction_index, val_energy, cond_energy, omegas)
    near = [ring(own, by) for by in (1, -1, 2)]
    beside = swap_x(own)
    near, beside, weight, meta = lax.optimization_barrier((near, beside, weight, meta))
    late = [ring(beside, by) for by in (1, -1)]
    far = [swap_x(near[2][:HALF]), ring(beside[HALF:], 2)]
    mine = [own] + near
    theirs = [swap_cores(v) for v in mine]
    total, following = early_product(meta, weight, mine, theirs)
    beside, far, total = lax.optimization_barrier((beside, far, total))
    others = [swap_cores(v) for v in [beside] + far]
    late, others = lax.optimization_barrier((late, others))
    mine += [beside] + late + far
    theirs += [others[0]] + [swap_cores(v) for v in late] + others[1:]
    return late_product(meta, weight, total, following, mine, theirs)


def solution(mesh):
    fine = Mesh(mesh.devices.reshape(SIZES), ALL)
    wide, narrow = ("xh", "z", "c"), ("xl", "y")
    return jax.shard_map(
        body,
        mesh=fine,
        in_specs=(P(wide + narrow, None), P(), P(), P(), P(), P()),
        out_specs=P(None, wide, narrow),
        check_vma=False,
    )
```
